128 devices in a mesh: region: 8 (over x, core), tm: 16 (over y, z).
Axes of the slice: x: 4, y: 4, z: 4, core: 2. Of those that a mesh axis runs over, the one named last changes fastest.
Arguments:
- x_start: float32 [4096], P('region'), parts along dimension 0, may hold values from -6 to 6
- ticks: int32 [4096], P(('region', 'tm')), parts along dimension 0, may hold values from 1 to 1280, as said below
- rates: float32 [4096], P('region'), parts along dimension 0, may hold values from 0.0001953125 to 0.1
- sensor_map: float32 [2048, 512], P('region'), parts along dimension 0, may hold values from -0.25 to 0.25
- coupling: int32 [16, 4], P('region'), parts along dimension 0, may hold values 0 or 1
- prior_var: float32 [4096], P('region'), parts along dimension 0, may hold values from 0.05 to 0.5
- noise_var: float32 [2048], P('region'), parts along dimension 0, may hold values from 1 to 4
- read_slab: int32 [262144, 1], P(('region', 'tm')), parts along dimension 0, may hold values from 0 to 15; in each aligned block of 2048 rows (0 to 2047, 2048 to 4095, ...) at most 256 rows name the same one
- read_offset: int32 [262144], P(('region', 'tm')), parts along dimension 0, may hold values from 0 to 31
- read_sensor: int32 [262144], P(('region', 'tm')), parts along dimension 0, may hold values from 0 to 15
- read_value: float32 [262144], P(('region', 'tm')), parts along dimension 0, may hold values from -6 to 6
Outputs:
- filtered: float32 [4096, 512], P(('region', 'tm')), parts along dimension 0
The draws below stay inside these ranges and needn't reach their ends.
There are 8 independent parts, one for each index of `region`. The reference program is written for one: setup_inputs(seed, part) draws one part's arguments, and reference() takes and returns one part's arrays. A program takes and returns all parts, laid end to end along the dimension named above; each array names one. Nothing has to cross between parts.
Inputs may be any that keep to these rules, and one draw needn't show every extreme that they name: `ticks`: strictly increasing; consecutive stamps, and the first stamp after tick 0, lie 1 to 4 ticks apart. `read_slab`: among the rows of one owner at most 256 name the same slab.
All inputs are finite; a program needn't handle non-finite values.
Results may differ from the reference program's by a relative error of at most 0.0003.
Values sent between devices are 32-bit elements; how exact they have to be, the bound alone decides.
No kernel may reach another device: no remote copies, remote signals or barrier semaphores. Data moves between devices by JAX's collectives and lax.ppermute only.
A program may use at most 128 MiB of HBM per device.

```python
import math
import jax
import jax.numpy as jnp
import numpy as np
from jax import lax

S = 512
NSENS = 256
BLOCK = 128
STAMP_DEV = 32
ROWS_DEV = 2048
STAMPS = 512
ROWS = 32768
CAP = 256
SENS_DEV = 16
N_TM = 16


def draw_ticks(key, part):
    key = jax.random.fold_in(key, 11)
    order = jax.random.permutation(key, STAMPS).astype(jnp.int32)
    spacing = 1 + order % 4
    return jnp.cumsum(spacing).astype(jnp.int32)


def place_ends(result, own_key, smallest, top_value):
    longest = result.shape.index(max(result.shape))
    spots = []
    for shift in (0, 1):
        where = [jax.random.randint(jax.random.fold_in(own_key, axis), (), 0, length) for axis, length in enumerate(result.shape)]
        where[longest] = (where[longest] + shift) % result.shape[longest]
        spots.append(tuple(where))
    return result.at[spots[0]].set(smallest).at[spots[1]].set(top_value)


def block_levels(stream_key, shape, pieces, least, largest):
    gain = 1.0
    for dim, shards_of in pieces:
        draws = jax.random.uniform(jax.random.fold_in(jax.random.fold_in(stream_key, 6), dim), (shards_of,), jnp.float32, least / len(pieces), largest / len(pieces))
        gain = gain * jnp.repeat(jnp.exp(draws), shape[dim] // shards_of).reshape((-1,) + (1,) * (len(shape) - 1 - dim))
    return gain


def shared_out(rng, own, number, rows, count, top, bound, skew):
    ranking = jax.random.permutation(rng, count)
    packed, common = shares(count, rows * top, bound, skew, True), shares(count, rows * top, bound, skew, False)
    places = jnp.arange(count)

    def named(lengths, offset_by):
        used = int((lengths > 0).sum())
        fixed = max(1, used // 4)
        passed = fixed + (places - fixed + offset_by * (used - fixed)) % max(1, count - fixed)
        return jnp.zeros((count,), jnp.int32).at[ranking[jnp.where(places < fixed, places, passed)]].set(jnp.asarray(lengths, jnp.int32))

    lengths = jnp.where(number % 4 == 0, named(packed, number // 4), named(common, number - number // 4 - 1))
    mixed = jax.random.permutation(jax.random.fold_in(own, 3), count)
    source_of, receiver = mixed[0:count // 2 * 2:2], mixed[1:count // 2 * 2:2]
    margin = jnp.minimum(lengths[source_of] - 1, bound - lengths[receiver]) // 2
    margin = jnp.where((source_of == ranking[0]) | (receiver == ranking[0]) | (lengths[receiver] == 0), 0, jnp.maximum(margin, 0))
    passed = jax.random.randint(jax.random.fold_in(own, 4), (count // 2,), 0, 1 << 20) % (margin + 1)
    lengths = lengths.at[source_of].add(-passed).at[receiver].add(passed)
    members = jnp.searchsorted(jnp.cumsum(lengths), jnp.arange(rows * top), side="right").astype(jnp.int32)
    grid = members.reshape(top, rows).T
    grid = grid[jax.random.permutation(jax.random.fold_in(own, 1), rows)]
    offset_by = jax.random.randint(jax.random.fold_in(own, 2), (rows, 1), 0, top)
    return jnp.take_along_axis(grid, (jnp.arange(top)[None, :] + offset_by) % top, axis=1)


def shares(count, total, bound, lean, full):
    loads = [(1 << 20) // math.isqrt(rank ** lean) + 1 for rank in range(1, count + 1)]
    largest = bound if full else min(bound, max(-(-total // count), total * loads[0] // sum(loads)))
    least = 1 if total - largest >= count - 1 else 0
    given, rest = [largest] + [least] * (count - 1), total - largest - least * (count - 1)
    while rest > 0:
        candidates = [i for i in range(1, count) if given[i] < largest] or [i for i in range(1, count) if given[i] < bound]
        pool, left = sum([loads[i] for i in candidates]), rest
        for i in candidates:
            addition = min(bound - given[i], max(1, left * loads[i] // pool), rest)
            given[i] = given[i] + addition
            rest = rest - addition
    return np.array(given)


def noise(stream_key, shape, scale, bound, cuts=(), held_as=jnp.bfloat16):
    result = jax.random.normal(stream_key, shape, jnp.float32) * scale
    if len(cuts) > 0:
        result = block_levels(stream_key, shape, cuts, -0.22, 0.18) * result
    return jnp.clip(result, min=-bound, max=bound).astype(held_as)


def setup_inputs(seed: int = 0, part: int = 0) -> dict:
    seeds = jax.random.split(jax.random.key(seed), 12)
    part_splits = jax.random.split(jax.random.fold_in(seeds[11], part), 12)
    x_start = noise(part_splits[0], (S,), 1.0, 6.0, (), jnp.float32)
    ticks = draw_ticks(jax.random.fold_in(jax.random.fold_in(seeds[11], part), 71), part)
    rates = jnp.clip(jnp.exp(jax.random.uniform(part_splits[2], (S,), jnp.float32, math.log(0.0001953125), math.log(0.1))), 0.0001953125, 0.1)
    sensor_map = noise(part_splits[3], (NSENS, S), S ** -0.5, 0.25, (), jnp.float32)
    coupling = place_ends((jax.random.randint(part_splits[4], (NSENS // BLOCK, S // BLOCK), 0, 4) < 3).astype(jnp.int32), jax.random.fold_in(part_splits[4], 1), 0, 1)
    prior_var = jnp.clip(jnp.exp(jax.random.uniform(part_splits[5], (S,), jnp.float32, math.log(0.05), math.log(0.5))), 0.05, 0.5)
    noise_var = jnp.clip(jnp.exp(jax.random.uniform(part_splits[6], (NSENS,), jnp.float32, math.log(1.0), math.log(4.0))), 1.0, 4.0)
    read_slab_keys = jax.random.split(jax.random.fold_in(part_splits[7], 1), ROWS // ROWS_DEV)
    read_slab_turns = jax.random.permutation(jax.random.fold_in(part_splits[7], 3), ROWS // ROWS_DEV)
    read_slab = jax.vmap(lambda own, number: shared_out(jax.random.fold_in(part_splits[7], 2), own, number, ROWS_DEV, N_TM, 1, CAP, 2))(read_slab_keys, read_slab_turns).reshape((ROWS, 1))
    read_offset = place_ends(jax.random.randint(part_splits[8], (ROWS,), 0, STAMP_DEV), jax.random.fold_in(part_splits[8], 1), 0, STAMP_DEV - 1).astype(jnp.int32)
    read_sensor = place_ends(jax.random.randint(part_splits[9], (ROWS,), 0, SENS_DEV), jax.random.fold_in(part_splits[9], 1), 0, SENS_DEV - 1).astype(jnp.int32)
    read_value = noise(part_splits[10], (ROWS,), 1.0, 6.0, ((0, 16),), jnp.float32)
    return dict(x_start=x_start, ticks=ticks, rates=rates, sensor_map=sensor_map, coupling=coupling, prior_var=prior_var, noise_var=noise_var, read_slab=read_slab, read_offset=read_offset, read_sensor=read_sensor, read_value=read_value)


def reference(x_start, ticks, rates, sensor_map, coupling, prior_var, noise_var, read_slab, read_offset, read_sensor, read_value):
    row_owner = (jnp.arange(ROWS) // ROWS_DEV).astype(jnp.int32)
    stamp = read_slab[:, 0] * STAMP_DEV + read_offset
    sensor = row_owner * SENS_DEV + read_sensor
    cell_id = (stamp * NSENS + sensor).astype(jnp.int32)
    sums = jnp.zeros((STAMPS * NSENS,), jnp.float32).at[cell_id].add(read_value.astype(jnp.float32))
    counts = jnp.zeros((STAMPS * NSENS,), jnp.float32).at[cell_id].add(jnp.ones((ROWS,), jnp.float32))
    sums = sums.reshape(STAMPS, NSENS)
    counts = counts.reshape(STAMPS, NSENS)
    observed = (counts > 0).astype(jnp.float32)
    readings = sums / jnp.maximum(counts, 1.0)
    pattern = jnp.repeat(jnp.repeat(coupling, BLOCK, 0), BLOCK, 1).astype(jnp.float32)
    hmat = sensor_map * pattern
    earlier = jnp.concatenate([jnp.zeros((1,), jnp.int32), ticks[:-1]])
    gap = (ticks - earlier).astype(jnp.float32)
    high = lax.Precision.HIGHEST

    def stepper(state, inputs):
        gap_now, seen_now, read_now = inputs
        moved = jnp.exp(-rates * gap_now) * state
        predicted = jnp.dot(hmat, moved, precision=high)
        weighted = seen_now * (read_now - predicted) / noise_var
        state = moved + prior_var * jnp.dot(weighted, hmat, precision=high)
        return state, state

    final, filtered = lax.scan(stepper, x_start.astype(jnp.float32), (gap, observed, readings))
    return filtered
```

```python
import jax
import jax.numpy as jnp
from jax import lax
from jax.experimental import pallas as pl
from jax.experimental.pallas import tpu as pltpu
from jax.sharding import PartitionSpec as P

BLOCK = 128
LANES = 128
SENS_DEV = 16
STAMP_DEV = 32
f32 = jnp.float32
bf16 = jnp.bfloat16


def split(value):
    high = value.astype(bf16)
    return high, (value - high.astype(f32)).astype(bf16)


def dot(left, right):
    return jnp.dot(left, right, preferred_element_type=f32)


def dot3(left, right):
    left_high, left_low = split(left)
    right_high, right_low = split(right)
    return dot(left_high, right_high) + (dot(left_low, right_high) + dot(left_high, right_low))


def total_over_sublanes(value):
    for shift in (4, 2, 1):
        value = value + pltpu.roll(value, shift, 0)
    return value


def kernel(
    slab_ref,
    coupling_ref,
    rows_ref,
    x_ref,
    rates_ref,
    map_ref,
    prior_ref,
    noise_ref,
    out_ref,
    hmat,
    sums,
    counts,
    seen,
    pushed,
    decay,
    tick,
    states,
    seen_a,
    seen_b,
):
    owners = rows_ref.shape[0]
    rows = 2048
    sensors, width = map_ref.shape
    chunks = owners * STAMP_DEV // LANES
    stamps = owners * STAMP_DEV

    eye = lax.broadcasted_iota(jnp.int32, (sensors, sensors), 0) == lax.broadcasted_iota(
        jnp.int32, (sensors, sensors), 1
    )
    noise = jnp.sum(jnp.where(eye, noise_ref[...], 0.0), axis=1, keepdims=True)
    scale = 1.0 / jnp.sqrt(noise)
    for i in range(sensors // BLOCK):
        for j in range(width // BLOCK):
            part = map_ref[i * BLOCK : (i + 1) * BLOCK, j * BLOCK : (j + 1) * BLOCK]
            present = coupling_ref[i, j].astype(f32)
            hmat[i * BLOCK : (i + 1) * BLOCK, j * BLOCK : (j + 1) * BLOCK] = (
                part * present * scale[i * BLOCK : (i + 1) * BLOCK]
            )

    tick[0:8, :] = jnp.zeros((8, LANES), f32)
    diagonal = lax.broadcasted_iota(jnp.int32, (STAMP_DEV, LANES), 0) == lax.broadcasted_iota(
        jnp.int32, (STAMP_DEV, LANES), 1
    )
    for q in range(owners):
        picked = jnp.where(diagonal, rows_ref[q, 0:1, rows:], 0.0)
        tick[8 + q * STAMP_DEV : 8 + (q + 1) * STAMP_DEV, :] = jnp.broadcast_to(
            jnp.sum(picked, axis=1, keepdims=True), (STAMP_DEV, LANES)
        )

    def decays(q, carry):
        at = pl.multiple_of(q * STAMP_DEV, STAMP_DEV)
        here = tick[pl.ds(8 + at, STAMP_DEV), :]
        gap = here - pltpu.roll(tick[pl.ds(at, STAMP_DEV + 8), :], STAMP_DEV + 1, 0)[:STAMP_DEV]
        gap = jnp.concatenate([gap] * (width // LANES), axis=1)
        decay[pl.ds(at, STAMP_DEV), :] = jnp.exp(-rates_ref[...] * gap)
        return carry

    lax.fori_loop(0, owners, decays, 0)

    row_index = lax.broadcasted_iota(jnp.int32, (chunks * SENS_DEV, rows), 0)
    stamp_index = lax.broadcasted_iota(jnp.int32, (LANES, rows), 0)

    def collect(q, carry):
        cell = rows_ref[q, 0:1, :rows].astype(jnp.int32)
        value = rows_ref[q, 1:2, :rows]
        stamp_hot = jnp.where(stamp_index == (cell & (LANES - 1)), 1.0, 0.0).astype(bf16)
        mine = row_index == (cell >> 7)
        high = value.astype(bf16).astype(f32)
        features = jnp.concatenate(
            [
                jnp.where(mine, high, 0.0).astype(bf16),
                jnp.where(mine, value - high, 0.0).astype(bf16),
                jnp.where(mine, 1.0, 0.0).astype(bf16),
            ],
            axis=0,
        )
        got = lax.dot_general(
            features, stamp_hot, (((1,), (1,)), ((), ())), preferred_element_type=f32
        )
        count = chunks * SENS_DEV
        for c in range(chunks):
            at = pl.multiple_of(c * sensors + q * SENS_DEV, SENS_DEV)
            low = c * SENS_DEV
            sums[pl.ds(at, SENS_DEV), :] = (
                got[low : low + SENS_DEV] + got[count + low : count + low + SENS_DEV]
            )
            counts[pl.ds(at, SENS_DEV), :] = got[2 * count + low : 2 * count + low + SENS_DEV]
        return carry

    lax.fori_loop(0, owners, collect, 0)

    for c in range(chunks):
        number = counts[c * sensors : (c + 1) * sensors, :]
        observed = number > 0.0
        reading = sums[c * sensors : (c + 1) * sensors, :] / jnp.maximum(number, 1.0)
        reading = jnp.where(observed, reading, 0.0) * scale
        seen[c * sensors : (c + 1) * sensors, :] = jnp.where(observed, 1.0, 0.0).astype(bf16)
        pushed[c * LANES : (c + 1) * LANES, :] = prior_ref[...] * dot3(reading.T, hmat[...])

    prior = jnp.broadcast_to(prior_ref[...], (8, width))
    sublane = lax.broadcasted_iota(jnp.int32, (LANES, LANES), 0)

    def fill(t, into):
        t = jnp.minimum(t, stamps - 1)
        at = pl.multiple_of((t // LANES) * sensors, sensors)
        pick = jnp.where(sublane == t % LANES, 1.0, 0.0).astype(bf16)
        into[...] = dot(seen[pl.ds(at, sensors), :], pick)

    def advance(t, state, seen_now):
        moved = state * jnp.broadcast_to(decay[pl.ds(t, 1), :], (8, width))
        base = moved + jnp.broadcast_to(pushed[pl.ds(t, 1), :], (8, width))
        total = [jnp.zeros((8, width), f32) for _ in range(2)]
        for i in range(sensors // 8):
            product = hmat[8 * i : 8 * i + 8, :] * moved
            product = (product[:, :128] + product[:, 128:256]) + (
                product[:, 256:384] + product[:, 384:]
            )
            predicted = jnp.broadcast_to(jnp.sum(product, axis=1, keepdims=True), (8, LANES))
            weighted = predicted * seen_now[8 * i : 8 * i + 8, :]
            total[i % 2] = total[i % 2] + jnp.concatenate([weighted] * 4, axis=1) * (
                hmat[8 * i : 8 * i + 8, :]
            )
        state = base - prior * total_over_sublanes(total[0] + total[1])
        states[pl.ds(t, 1), :] = state[:1]
        return state

    def pair(k, state):
        fill(2 * k + 1, seen_b)
        state = advance(2 * k, state, seen_a)
        fill(2 * k + 2, seen_a)
        return advance(2 * k + 1, state, seen_b)

    fill(0, seen_a)
    slab = slab_ref[0]
    lax.fori_loop(
        0, (slab + 1) * (STAMP_DEV // 2), pair, jnp.broadcast_to(x_ref[...], (8, width))
    )
    out_ref[...] = states[pl.ds(pl.multiple_of(slab * STAMP_DEV, STAMP_DEV), STAMP_DEV), :]


def gathered(value, axis):
    count = lax.axis_size(axis)
    copies = jnp.broadcast_to(value[None], (count,) + value.shape)
    return lax.all_to_all(copies, axis, split_axis=0, concat_axis=0, tiled=True)


def shards(
    x_start,
    ticks,
    rates,
    sensor_map,
    coupling,
    prior_var,
    noise_var,
    read_slab,
    read_offset,
    read_sensor,
    read_value,
):
    slab = lax.axis_index("tm").astype(jnp.int32)
    owners = lax.axis_size("tm")
    sensors, width = sensor_map.shape
    per_chunk = LANES // STAMP_DEV
    reads = read_slab[:, 0]
    cell = ((reads // per_chunk) * SENS_DEV + read_sensor) * LANES + (
        reads % per_chunk
    ) * STAMP_DEV + read_offset
    tail = jnp.zeros((LANES - STAMP_DEV,), f32)
    first = jnp.concatenate([cell.astype(f32), ticks.astype(f32), tail])
    second = jnp.concatenate([read_value, jnp.zeros((LANES,), f32)])
    rows = gathered(jnp.stack([first, second]), "tm")
    stamps = owners * STAMP_DEV
    chunks = stamps // LANES
    vmem, smem = pl.BlockSpec(memory_space=pltpu.VMEM), pl.BlockSpec(memory_space=pltpu.SMEM)
    return pl.pallas_call(
        kernel,
        out_shape=jax.ShapeDtypeStruct((STAMP_DEV, width), f32),
        in_specs=[smem, smem] + [vmem] * 6,
        out_specs=vmem,
        scratch_shapes=[
            pltpu.VMEM((sensors, width), f32),
            pltpu.VMEM((chunks * sensors, LANES), f32),
            pltpu.VMEM((chunks * sensors, LANES), f32),
            pltpu.VMEM((chunks * sensors, LANES), bf16),
            pltpu.VMEM((stamps, width), f32),
            pltpu.VMEM((stamps, width), f32),
            pltpu.VMEM((stamps + 8, LANES), f32),
            pltpu.VMEM((stamps, width), f32),
            pltpu.VMEM((sensors, LANES), f32),
            pltpu.VMEM((sensors, LANES), f32),
        ],
        compiler_params=pltpu.CompilerParams(vmem_limit_bytes=40 * 2**20),
    )(
        slab[None],
        coupling,
        rows,
        x_start[None],
        rates[None],
        sensor_map,
        prior_var[None],
        noise_var[None],
    )


def solution(mesh):
    return jax.shard_map(
        shards,
        mesh=mesh,
        in_specs=(
            P("region"),
            P(("region", "tm")),
            P("region"),
            P("region", None),
            P("region", None),
            P("region"),
            P("region"),
            P(("region", "tm"), None),
            P(("region", "tm")),
            P(("region", "tm")),
            P(("region", "tm")),
        ),
        out_specs=P(("region", "tm"), None),
        check_vma=False,
    )
```

```python
import jax
import jax.numpy as jnp
from jax import lax
from jax.experimental import pallas as pl
from jax.experimental.pallas import tpu as pltpu
from jax.sharding import PartitionSpec as P

BLOCK = 128
LANES = 128
SENS_DEV = 16
STAMP_DEV = 32
GROUP = 8
KEPT = 112
BATCH = 4
f32 = jnp.float32
bf16 = jnp.bfloat16


def split(value):
    high = value.astype(bf16)
    return high, (value - high.astype(f32)).astype(bf16)


def dot(left, right):
    return jnp.dot(left, right, preferred_element_type=f32)


def dot3(left, right):
    left_high, left_low = split(left)
    right_high, right_low = split(right)
    return dot(left_high, right_high) + (dot(left_low, right_high) + dot(left_high, right_low))


def total_over_sublanes(value):
    for shift in (4, 2, 1):
        value = value + pltpu.roll(value, shift, 0)
    return value


def kernel(
    slab_ref,
    coupling_ref,
    rows_ref,
    x_ref,
    rates_ref,
    map_ref,
    prior_ref,
    noise_ref,
    out_ref,
    hmat,
    sums,
    counts,
    seen,
    pushed,
    decay,
    tick,
    states,
    seen_a,
    seen_b,
    rank,
    table,
    scalars,
    arrived,
    halves,
    held_a,
    held_b,
):
    owners = rows_ref.shape[0]
    rows = 2048
    sensors, width = map_ref.shape
    chunks = owners * STAMP_DEV // LANES
    stamps = owners * STAMP_DEV

    eye = lax.broadcasted_iota(jnp.int32, (sensors, sensors), 0) == lax.broadcasted_iota(
        jnp.int32, (sensors, sensors), 1
    )
    noise = jnp.sum(jnp.where(eye, noise_ref[...], 0.0), axis=1, keepdims=True)
    scale = 1.0 / jnp.sqrt(noise)
    for i in range(sensors // BLOCK):
        for j in range(width // BLOCK):
            part = map_ref[i * BLOCK : (i + 1) * BLOCK, j * BLOCK : (j + 1) * BLOCK]
            present = coupling_ref[i, j].astype(f32)
            hmat[i * BLOCK : (i + 1) * BLOCK, j * BLOCK : (j + 1) * BLOCK] = (
                part * present * scale[i * BLOCK : (i + 1) * BLOCK]
            )

    tick[0:8, :] = jnp.zeros((8, LANES), f32)
    diagonal = lax.broadcasted_iota(jnp.int32, (STAMP_DEV, LANES), 0) == lax.broadcasted_iota(
        jnp.int32, (STAMP_DEV, LANES), 1
    )
    for q in range(owners):
        picked = jnp.where(diagonal, rows_ref[q, 0:1, rows:], 0.0)
        tick[8 + q * STAMP_DEV : 8 + (q + 1) * STAMP_DEV, :] = jnp.broadcast_to(
            jnp.sum(picked, axis=1, keepdims=True), (STAMP_DEV, LANES)
        )

    def decays(q, carry):
        at = pl.multiple_of(q * STAMP_DEV, STAMP_DEV)
        here = tick[pl.ds(8 + at, STAMP_DEV), :]
        gap = here - pltpu.roll(tick[pl.ds(at, STAMP_DEV + 8), :], STAMP_DEV + 1, 0)[:STAMP_DEV]
        gap = jnp.concatenate([gap] * (width // LANES), axis=1)
        decay[pl.ds(at, STAMP_DEV), :] = jnp.exp(-rates_ref[...] * gap)
        return carry

    lax.fori_loop(0, owners, decays, 0)

    row_index = lax.broadcasted_iota(jnp.int32, (chunks * SENS_DEV, rows), 0)
    stamp_index = lax.broadcasted_iota(jnp.int32, (LANES, rows), 0)

    def collect(q, carry):
        cell = rows_ref[q, 0:1, :rows].astype(jnp.int32)
        value = rows_ref[q, 1:2, :rows]
        stamp_hot = jnp.where(stamp_index == (cell & (LANES - 1)), 1.0, 0.0).astype(bf16)
        mine = row_index == (cell >> 7)
        high = value.astype(bf16).astype(f32)
        features = jnp.concatenate(
            [
                jnp.where(mine, high, 0.0).astype(bf16),
                jnp.where(mine, value - high, 0.0).astype(bf16),
                jnp.where(mine, 1.0, 0.0).astype(bf16),
            ],
            axis=0,
        )
        got = lax.dot_general(
            features, stamp_hot, (((1,), (1,)), ((), ())), preferred_element_type=f32
        )
        count = chunks * SENS_DEV
        for c in range(chunks):
            at = pl.multiple_of(c * sensors + q * SENS_DEV, SENS_DEV)
            low = c * SENS_DEV
            sums[pl.ds(at, SENS_DEV), :] = (
                got[low : low + SENS_DEV] + got[count + low : count + low + SENS_DEV]
            )
            counts[pl.ds(at, SENS_DEV), :] = got[2 * count + low : 2 * count + low + SENS_DEV]
        return carry

    lax.fori_loop(0, owners, collect, 0)

    for c in range(chunks):
        number = counts[c * sensors : (c + 1) * sensors, :]
        observed = number > 0.0
        reading = sums[c * sensors : (c + 1) * sensors, :] / jnp.maximum(number, 1.0)
        reading = jnp.where(observed, reading, 0.0) * scale
        seen[c * sensors : (c + 1) * sensors, :] = jnp.where(observed, 1.0, 0.0).astype(bf16)
        pushed[c * LANES : (c + 1) * LANES, :] = prior_ref[...] * dot3(reading.T, hmat[...])

    below = lax.broadcasted_iota(jnp.int32, (sensors, sensors), 0) < lax.broadcasted_iota(
        jnp.int32, (sensors, sensors), 1
    )
    below = jnp.where(below, 1.0, 0.0).astype(bf16)
    table[...] = jnp.zeros(table.shape, jnp.int32)
    for c in range(chunks):
        observed = jnp.where(counts[c * sensors : (c + 1) * sensors, :] > 0.0, 1.0, 0.0)
        table[c : c + 1, :] = jnp.sum(observed, axis=0, keepdims=True).astype(jnp.int32)
        observed = observed.T
        place = dot(observed.astype(bf16), below)
        rank[c * LANES : (c + 1) * LANES, :] = jnp.where(observed > 0.0, place, 512.0)
    copy = pltpu.make_async_copy(table, scalars, arrived)
    copy.start()
    high, low = split(hmat[...])
    halves[:sensors, :] = high
    halves[sensors:, :] = low
    copy.wait()

    prior = jnp.broadcast_to(prior_ref[...], (8, width))
    sublane = lax.broadcasted_iota(jnp.int32, (LANES, LANES), 0)
    slot = lax.broadcasted_iota(jnp.int32, (KEPT, sensors), 0).astype(f32).astype(bf16)
    one, zero = jnp.ones((), bf16), jnp.zeros((), bf16)

    def fill(t, into):
        t = jnp.minimum(t, stamps - 1)
        at = pl.multiple_of((t // LANES) * sensors, sensors)
        pick = jnp.where(sublane == t % LANES, 1.0, 0.0).astype(bf16)
        into[...] = dot(seen[pl.ds(at, sensors), :], pick)

    def advance(t, moved, chosen, seen_now):
        base = moved + jnp.broadcast_to(pushed[pl.ds(t, 1), :], (8, width))
        after = jnp.broadcast_to(decay[pl.ds(jnp.minimum(t + 1, stamps - 1), 1), :], (8, width))
        base_after, prior_after = base * after, prior * after
        total = [jnp.zeros((8, width), f32) for _ in range(2)]
        matrix, start, rows_used = chosen
        for i in range(rows_used // 8):
            at = slice(start + 8 * i, start + 8 * i + 8)
            product = matrix[at, :] * moved
            product = (product[:, :128] + product[:, 128:256]) + (
                product[:, 256:384] + product[:, 384:]
            )
            weighted = jnp.broadcast_to(jnp.sum(product, axis=1, keepdims=True), (8, LANES))
            if seen_now is not None:
                weighted = weighted * seen_now[8 * i : 8 * i + 8, :]
            total[i % 2] = total[i % 2] + jnp.concatenate([weighted] * 4, axis=1) * matrix[at, :]
        change = total_over_sublanes(total[0] + total[1])
        states[pl.ds(t, 1), :] = (base - prior * change)[:1]
        return base_after - prior_after * change

    def prepare(group, into):
        first = pl.multiple_of(group * GROUP, GROUP)
        ranks = rank[pl.ds(first, GROUP), :]
        for j in range(0, GROUP, BATCH):
            pick = jnp.concatenate(
                [
                    jnp.where(
                        slot == jnp.broadcast_to(ranks[j + k : j + k + 1], (KEPT, sensors)).astype(bf16),
                        one,
                        zero,
                    )
                    for k in range(BATCH)
                ],
                axis=0,
            )
            into[KEPT * j : KEPT * (j + BATCH), :] = dot(
                jnp.concatenate([pick, pick], axis=1), halves[...]
            )

    def on_all(group, moved, fill_next):
        first = group * GROUP
        for j in range(GROUP):
            if j + 1 < GROUP or fill_next:
                fill(first + j + 1, seen_a if j % 2 else seen_b)
            moved = advance(
                first + j, moved, (hmat, 0, sensors), seen_b if j % 2 else seen_a
            )
        return moved

    def on_seen(group, moved, held):
        for j in range(GROUP):
            moved = advance(group * GROUP + j, moved, (held, KEPT * j, KEPT), None)
        return moved

    def few_seen(group):
        most = jnp.int32(0)
        for j in range(GROUP):
            t = group * GROUP + j
            most = jnp.maximum(most, scalars[t // LANES, t % LANES])
        return most <= KEPT

    slab = slab_ref[0]
    mine = slab * (STAMP_DEV // GROUP)

    def step(group, moved, held, ahead):
        after = group + 1
        case = jnp.where(few_seen(group), 2, 0) + jnp.where(
            (after < mine) & few_seen(jnp.minimum(after, stamps // GROUP - 1)), 1, 0
        )

        def branch(few, few_after):
            def run(moved):
                if few_after:
                    prepare(after, ahead)
                if few:
                    if not few_after:
                        fill(after * GROUP, seen_a)
                    return on_seen(group, moved, held)
                return on_all(group, moved, not few_after)

            return run

        return lax.switch(
            case, [branch(False, False), branch(False, True), branch(True, False), branch(True, True)], moved
        )

    def two_groups(k, moved):
        moved = step(2 * k, moved, held_a, held_b)
        return step(2 * k + 1, moved, held_b, held_a)

    prepare(jnp.int32(0), held_a)
    fill(jnp.int32(0), seen_a)
    moved = jnp.broadcast_to(x_ref[...] * decay[0:1, :], (8, width))
    moved = lax.fori_loop(0, mine // 2, two_groups, moved)
    lax.fori_loop(
        mine, mine + STAMP_DEV // GROUP, lambda group, moved: on_all(group, moved, True), moved
    )
    out_ref[...] = states[pl.ds(pl.multiple_of(slab * STAMP_DEV, STAMP_DEV), STAMP_DEV), :]


def payload(slab_ref, offset_ref, sensor_ref, value_ref, ticks_ref, out_ref):
    copies, count = out_ref.shape[0], value_ref.shape[1]
    slab = slab_ref[...]
    per_chunk = LANES // STAMP_DEV
    chunk, within = slab // per_chunk, slab % per_chunk
    cell = (chunk * SENS_DEV + sensor_ref[...]) * LANES + within * STAMP_DEV + offset_ref[...]
    cell, value = cell.astype(f32), value_ref[...]
    tick = jnp.concatenate(
        [ticks_ref[...].astype(f32), jnp.zeros((1, LANES - STAMP_DEV), f32)], axis=1
    )
    for d in range(copies):
        out_ref[d, 0:1, :count] = cell
        out_ref[d, 1:2, :count] = value
        out_ref[d, 0:1, count:] = tick
        out_ref[d, 1:2, count:] = jnp.zeros((1, LANES), f32)


def shards(
    x_start,
    ticks,
    rates,
    sensor_map,
    coupling,
    prior_var,
    noise_var,
    read_slab,
    read_offset,
    read_sensor,
    read_value,
):
    slab = lax.axis_index("tm").astype(jnp.int32)
    owners = lax.axis_size("tm")
    sensors, width = sensor_map.shape
    count = read_value.shape[0]
    copies = pl.pallas_call(
        payload,
        out_shape=jax.ShapeDtypeStruct((owners, 2, count + LANES), f32),
    )(
        read_slab.reshape(1, count),
        read_offset[None],
        read_sensor[None],
        read_value[None],
        ticks[None],
    )
    rows = lax.all_to_all(copies, "tm", split_axis=0, concat_axis=0, tiled=True)
    stamps = owners * STAMP_DEV
    chunks = stamps // LANES
    vmem, smem = pl.BlockSpec(memory_space=pltpu.VMEM), pl.BlockSpec(memory_space=pltpu.SMEM)
    return pl.pallas_call(
        kernel,
        out_shape=jax.ShapeDtypeStruct((STAMP_DEV, width), f32),
        in_specs=[smem, smem] + [vmem] * 6,
        out_specs=vmem,
        scratch_shapes=[
            pltpu.VMEM((sensors, width), f32),
            pltpu.VMEM((chunks * sensors, LANES), f32),
            pltpu.VMEM((chunks * sensors, LANES), f32),
            pltpu.VMEM((chunks * sensors, LANES), bf16),
            pltpu.VMEM((stamps, width), f32),
            pltpu.VMEM((stamps, width), f32),
            pltpu.VMEM((stamps + 8, LANES), f32),
            pltpu.VMEM((stamps, width), f32),
            pltpu.VMEM((sensors, LANES), f32),
            pltpu.VMEM((sensors, LANES), f32),
            pltpu.VMEM((stamps, sensors), f32),
            pltpu.VMEM((8, LANES), jnp.int32),
            pltpu.SMEM((8, LANES), jnp.int32),
            pltpu.SemaphoreType.DMA,
            pltpu.VMEM((2 * sensors, width), bf16),
            pltpu.VMEM((GROUP * KEPT, width), f32),
            pltpu.VMEM((GROUP * KEPT, width), f32),
        ],
        compiler_params=pltpu.CompilerParams(vmem_limit_bytes=40 * 2**20),
    )(
        slab[None],
        coupling,
        rows,
        x_start[None],
        rates[None],
        sensor_map,
        prior_var[None],
        noise_var[None],
    )


def solution(mesh):
    return jax.shard_map(
        shards,
        mesh=mesh,
        in_specs=(
            P("region"),
            P(("region", "tm")),
            P("region"),
            P("region", None),
            P("region", None),
            P("region"),
            P("region"),
            P(("region", "tm"), None),
            P(("region", "tm")),
            P(("region", "tm")),
            P(("region", "tm")),
        ),
        out_specs=P(("region", "tm"), None),
        check_vma=False,
    )
```

```python
import jax
import jax.numpy as jnp
from jax import lax
from jax.experimental import pallas as pl
from jax.experimental.pallas import tpu as pltpu
from jax.sharding import PartitionSpec as P

BLOCK = 128
LANES = 128
SENS_DEV = 16
STAMP_DEV = 32
GROUP = 8
KEPT = 112
BATCH = 2
f32 = jnp.float32
bf16 = jnp.bfloat16


def split(value):
    high = value.astype(bf16)
    return high, (value - high.astype(f32)).astype(bf16)


def dot(left, right):
    return jnp.dot(left, right, preferred_element_type=f32)


def dot3(left, right):
    left_high, left_low = split(left)
    right_high, right_low = split(right)
    return dot(left_high, right_high) + (dot(left_low, right_high) + dot(left_high, right_low))


def total_over_sublanes(value):
    for shift in (4, 2, 1):
        value = value + pltpu.roll(value, shift, 0)
    return value


def kernel(
    slab_ref,
    coupling_ref,
    rows_ref,
    x_ref,
    rates_ref,
    map_ref,
    prior_ref,
    noise_ref,
    out_ref,
    hmat,
    sums,
    counts,
    seen,
    pushed,
    decay,
    tick,
    states,
    seen_a,
    seen_b,
    rank,
    table,
    scalars,
    arrived,
    halves,
    held_a,
    held_b,
):
    owners = rows_ref.shape[0]
    rows = 2048
    sensors, width = map_ref.shape
    chunks = owners * STAMP_DEV // LANES
    stamps = owners * STAMP_DEV

    eye = lax.broadcasted_iota(jnp.int32, (sensors, sensors), 0) == lax.broadcasted_iota(
        jnp.int32, (sensors, sensors), 1
    )
    noise = jnp.sum(jnp.where(eye, noise_ref[...], 0.0), axis=1, keepdims=True)
    scale = 1.0 / jnp.sqrt(noise)
    for i in range(sensors // BLOCK):
        for j in range(width // BLOCK):
            part = map_ref[i * BLOCK : (i + 1) * BLOCK, j * BLOCK : (j + 1) * BLOCK]
            present = coupling_ref[i, j].astype(f32)
            hmat[i * BLOCK : (i + 1) * BLOCK, j * BLOCK : (j + 1) * BLOCK] = (
                part * present * scale[i * BLOCK : (i + 1) * BLOCK]
            )

    tick[0:8, :] = jnp.zeros((8, LANES), f32)
    diagonal = lax.broadcasted_iota(jnp.int32, (STAMP_DEV, LANES), 0) == lax.broadcasted_iota(
        jnp.int32, (STAMP_DEV, LANES), 1
    )
    for q in range(owners):
        picked = jnp.where(diagonal, rows_ref[q, 0:1, rows:], 0.0)
        tick[8 + q * STAMP_DEV : 8 + (q + 1) * STAMP_DEV, :] = jnp.broadcast_to(
            jnp.sum(picked, axis=1, keepdims=True), (STAMP_DEV, LANES)
        )

    def decays(q, carry):
        at = pl.multiple_of(q * STAMP_DEV, STAMP_DEV)
        here = tick[pl.ds(8 + at, STAMP_DEV), :]
        gap = here - pltpu.roll(tick[pl.ds(at, STAMP_DEV + 8), :], STAMP_DEV + 1, 0)[:STAMP_DEV]
        gap = jnp.concatenate([gap] * (width // LANES), axis=1)
        decay[pl.ds(at, STAMP_DEV), :] = jnp.exp(-rates_ref[...] * gap)
        return carry

    lax.fori_loop(0, owners, decays, 0)

    row_index = lax.broadcasted_iota(jnp.int32, (chunks * SENS_DEV, rows), 0)
    stamp_index = lax.broadcasted_iota(jnp.int32, (LANES, rows), 0)

    def collect(q, carry):
        cell = rows_ref[q, 0:1, :rows].astype(jnp.int32)
        value = rows_ref[q, 1:2, :rows]
        stamp_hot = jnp.where(stamp_index == (cell & (LANES - 1)), 1.0, 0.0).astype(bf16)
        mine = row_index == (cell >> 7)
        high = value.astype(bf16).astype(f32)
        features = jnp.concatenate(
            [
                jnp.where(mine, high, 0.0).astype(bf16),
                jnp.where(mine, value - high, 0.0).astype(bf16),
                jnp.where(mine, 1.0, 0.0).astype(bf16),
            ],
            axis=0,
        )
        got = lax.dot_general(
            features, stamp_hot, (((1,), (1,)), ((), ())), preferred_element_type=f32
        )
        count = chunks * SENS_DEV
        for c in range(chunks):
            at = pl.multiple_of(c * sensors + q * SENS_DEV, SENS_DEV)
            low = c * SENS_DEV
            sums[pl.ds(at, SENS_DEV), :] = (
                got[low : low + SENS_DEV] + got[count + low : count + low + SENS_DEV]
            )
            counts[pl.ds(at, SENS_DEV), :] = got[2 * count + low : 2 * count + low + SENS_DEV]
        return carry

    lax.fori_loop(0, owners, collect, 0)

    for c in range(chunks):
        number = counts[c * sensors : (c + 1) * sensors, :]
        observed = number > 0.0
        reading = sums[c * sensors : (c + 1) * sensors, :] / jnp.maximum(number, 1.0)
        reading = jnp.where(observed, reading, 0.0) * scale
        seen[c * sensors : (c + 1) * sensors, :] = jnp.where(observed, 1.0, 0.0).astype(bf16)
        pushed[c * LANES : (c + 1) * LANES, :] = prior_ref[...] * dot3(reading.T, hmat[...])

    below = lax.broadcasted_iota(jnp.int32, (sensors, sensors), 0) < lax.broadcasted_iota(
        jnp.int32, (sensors, sensors), 1
    )
    below = jnp.where(below, 1.0, 0.0).astype(bf16)
    table[...] = jnp.zeros(table.shape, jnp.int32)
    for c in range(chunks):
        observed = jnp.where(counts[c * sensors : (c + 1) * sensors, :] > 0.0, 1.0, 0.0)
        table[c : c + 1, :] = jnp.sum(observed, axis=0, keepdims=True).astype(jnp.int32)
        observed = observed.T
        place = dot(observed.astype(bf16), below)
        rank[c * LANES : (c + 1) * LANES, :] = jnp.where(observed > 0.0, place, 512.0)
    copy = pltpu.make_async_copy(table, scalars, arrived)
    copy.start()
    high, low = split(hmat[...])
    halves[:sensors, :] = high
    halves[sensors:, :] = low
    copy.wait()

    prior = jnp.broadcast_to(prior_ref[...], (8, width))
    sublane = lax.broadcasted_iota(jnp.int32, (LANES, LANES), 0)
    slot = lax.broadcasted_iota(jnp.int32, (KEPT, sensors), 0).astype(f32).astype(bf16)
    one, zero = jnp.ones((), bf16), jnp.zeros((), bf16)

    def fill(t, into):
        t = jnp.minimum(t, stamps - 1)
        at = pl.multiple_of((t // LANES) * sensors, sensors)
        pick = jnp.where(sublane == t % LANES, 1.0, 0.0).astype(bf16)
        into[...] = dot(seen[pl.ds(at, sensors), :], pick)

    def advance(t, moved, chosen, seen_now):
        base = moved + jnp.broadcast_to(pushed[pl.ds(t, 1), :], (8, width))
        after = jnp.broadcast_to(decay[pl.ds(jnp.minimum(t + 1, stamps - 1), 1), :], (8, width))
        base_after, prior_after = base * after, prior * after
        total = [jnp.zeros((8, width), f32) for _ in range(2)]
        matrix, start, rows_used = chosen
        for i in range(rows_used // 8):
            at = slice(start + 8 * i, start + 8 * i + 8)
            product = matrix[at, :] * moved
            product = (product[:, :128] + product[:, 128:256]) + (
                product[:, 256:384] + product[:, 384:]
            )
            weighted = jnp.broadcast_to(jnp.sum(product, axis=1, keepdims=True), (8, LANES))
            if seen_now is not None:
                weighted = weighted * seen_now[8 * i : 8 * i + 8, :]
            total[i % 2] = total[i % 2] + jnp.concatenate([weighted] * 4, axis=1) * matrix[at, :]
        change = total_over_sublanes(total[0] + total[1])
        states[pl.ds(t, 1), :] = (base - prior * change)[:1]
        return base_after - prior_after * change

    def prepare(group, into, steps=range(0, GROUP, BATCH)):
        first = pl.multiple_of(group * GROUP, GROUP)
        ranks = rank[pl.ds(first, GROUP), :]
        for j in steps:
            pick = jnp.concatenate(
                [
                    jnp.where(
                        slot == jnp.broadcast_to(ranks[j + k : j + k + 1], (KEPT, sensors)).astype(bf16),
                        one,
                        zero,
                    )
                    for k in range(BATCH)
                ],
                axis=0,
            )
            into[KEPT * j : KEPT * (j + BATCH), :] = dot(
                jnp.concatenate([pick, pick], axis=1), halves[...]
            )

    def on_all(group, moved, ahead):
        first = group * GROUP
        for j in range(GROUP):
            if ahead is not None and j % BATCH == 0:
                prepare(group + 1, ahead, (j,))
            if j + 1 < GROUP or ahead is None:
                fill(first + j + 1, seen_a if j % 2 else seen_b)
            moved = advance(
                first + j, moved, (hmat, 0, sensors), seen_b if j % 2 else seen_a
            )
        return moved

    def on_seen(group, moved, held, ahead):
        for j in range(GROUP):
            if ahead is not None and j % BATCH == 0:
                prepare(group + 1, ahead, (j,))
            moved = advance(group * GROUP + j, moved, (held, KEPT * j, KEPT), None)
        return moved

    def few_seen(group):
        most = jnp.int32(0)
        for j in range(GROUP):
            t = group * GROUP + j
            most = jnp.maximum(most, scalars[t // LANES, t % LANES])
        return most <= KEPT

    slab = slab_ref[0]
    mine = slab * (STAMP_DEV // GROUP)

    def step(group, moved, held, ahead):
        after = group + 1
        case = jnp.where(few_seen(group), 2, 0) + jnp.where(
            (after < mine) & few_seen(jnp.minimum(after, stamps // GROUP - 1)), 1, 0
        )

        def branch(few, few_after):
            def run(moved):
                into = ahead if few_after else None
                if few:
                    if not few_after:
                        fill(after * GROUP, seen_a)
                    return on_seen(group, moved, held, into)
                return on_all(group, moved, into)

            return run

        return lax.switch(
            case, [branch(False, False), branch(False, True), branch(True, False), branch(True, True)], moved
        )

    def two_groups(k, moved):
        moved = step(2 * k, moved, held_a, held_b)
        return step(2 * k + 1, moved, held_b, held_a)

    prepare(jnp.int32(0), held_a)
    fill(jnp.int32(0), seen_a)
    moved = jnp.broadcast_to(x_ref[...] * decay[0:1, :], (8, width))
    moved = lax.fori_loop(0, mine // 2, two_groups, moved)
    lax.fori_loop(
        mine, mine + STAMP_DEV // GROUP, lambda group, moved: on_all(group, moved, None), moved
    )
    out_ref[...] = states[pl.ds(pl.multiple_of(slab * STAMP_DEV, STAMP_DEV), STAMP_DEV), :]


def payload(slab_ref, offset_ref, sensor_ref, value_ref, ticks_ref, out_ref):
    copies, count = out_ref.shape[0], value_ref.shape[1]
    slab = slab_ref[...]
    per_chunk = LANES // STAMP_DEV
    chunk, within = slab // per_chunk, slab % per_chunk
    cell = (chunk * SENS_DEV + sensor_ref[...]) * LANES + within * STAMP_DEV + offset_ref[...]
    cell, value = cell.astype(f32), value_ref[...]
    tick = jnp.concatenate(
        [ticks_ref[...].astype(f32), jnp.zeros((1, LANES - STAMP_DEV), f32)], axis=1
    )
    for d in range(copies):
        out_ref[d, 0:1, :count] = cell
        out_ref[d, 1:2, :count] = value
        out_ref[d, 0:1, count:] = tick
        out_ref[d, 1:2, count:] = jnp.zeros((1, LANES), f32)


def shards(
    x_start,
    ticks,
    rates,
    sensor_map,
    coupling,
    prior_var,
    noise_var,
    read_slab,
    read_offset,
    read_sensor,
    read_value,
):
    slab = lax.axis_index("tm").astype(jnp.int32)
    owners = lax.axis_size("tm")
    sensors, width = sensor_map.shape
    count = read_value.shape[0]
    copies = pl.pallas_call(
        payload,
        out_shape=jax.ShapeDtypeStruct((owners, 2, count + LANES), f32),
    )(
        read_slab.reshape(1, count),
        read_offset[None],
        read_sensor[None],
        read_value[None],
        ticks[None],
    )
    rows = lax.all_to_all(copies, "tm", split_axis=0, concat_axis=0, tiled=True)
    stamps = owners * STAMP_DEV
    chunks = stamps // LANES
    vmem, smem = pl.BlockSpec(memory_space=pltpu.VMEM), pl.BlockSpec(memory_space=pltpu.SMEM)
    return pl.pallas_call(
        kernel,
        out_shape=jax.ShapeDtypeStruct((STAMP_DEV, width), f32),
        in_specs=[smem, smem] + [vmem] * 6,
        out_specs=vmem,
        scratch_shapes=[
            pltpu.VMEM((sensors, width), f32),
            pltpu.VMEM((chunks * sensors, LANES), f32),
            pltpu.VMEM((chunks * sensors, LANES), f32),
            pltpu.VMEM((chunks * sensors, LANES), bf16),
            pltpu.VMEM((stamps, width), f32),
            pltpu.VMEM((stamps, width), f32),
            pltpu.VMEM((stamps + 8, LANES), f32),
            pltpu.VMEM((stamps, width), f32),
            pltpu.VMEM((sensors, LANES), f32),
            pltpu.VMEM((sensors, LANES), f32),
            pltpu.VMEM((stamps, sensors), f32),
            pltpu.VMEM((8, LANES), jnp.int32),
            pltpu.SMEM((8, LANES), jnp.int32),
            pltpu.SemaphoreType.DMA,
            pltpu.VMEM((2 * sensors, width), bf16),
            pltpu.VMEM((GROUP * KEPT, width), f32),
            pltpu.VMEM((GROUP * KEPT, width), f32),
        ],
        compiler_params=pltpu.CompilerParams(vmem_limit_bytes=40 * 2**20),
    )(
        slab[None],
        coupling,
        rows,
        x_start[None],
        rates[None],
        sensor_map,
        prior_var[None],
        noise_var[None],
    )


def solution(mesh):
    return jax.shard_map(
        shards,
        mesh=mesh,
        in_specs=(
            P("region"),
            P(("region", "tm")),
            P("region"),
            P("region", None),
            P("region", None),
            P("region"),
            P("region"),
            P(("region", "tm"), None),
            P(("region", "tm")),
            P(("region", "tm")),
            P(("region", "tm")),
        ),
        out_specs=P(("region", "tm"), None),
        check_vma=False,
    )
```

```python
import jax
import jax.numpy as jnp
from jax import lax
from jax.experimental import pallas as pl
from jax.experimental.pallas import tpu as pltpu
from jax.sharding import PartitionSpec as P

BLOCK = 128
LANES = 128
SENS_DEV = 16
STAMP_DEV = 32
GROUP = 8
KEPT = 112
BATCH = 2
f32 = jnp.float32
bf16 = jnp.bfloat16


def split(value):
    high = value.astype(bf16)
    return high, (value - high.astype(f32)).astype(bf16)


def dot(left, right):
    return jnp.dot(left, right, preferred_element_type=f32)


def dot3(left, right):
    left_high, left_low = split(left)
    right_high, right_low = split(right)
    return dot(left_high, right_high) + (dot(left_low, right_high) + dot(left_high, right_low))


def total_over_sublanes(value):
    for shift in (4, 2, 1):
        value = value + pltpu.roll(value, shift, 0)
    return value


def kernel(
    slab_ref,
    coupling_ref,
    rows_ref,
    x_ref,
    rates_ref,
    map_ref,
    prior_ref,
    noise_ref,
    out_ref,
    hmat,
    sums,
    counts,
    seen,
    pushed,
    decay,
    tick,
    states,
    seen_a,
    seen_b,
    rank,
    table,
    scalars,
    arrived,
    halves,
    held_a,
    held_b,
):
    owners = rows_ref.shape[0]
    rows = 2048
    sensors, width = map_ref.shape
    chunks = owners * STAMP_DEV // LANES
    stamps = owners * STAMP_DEV

    eye = lax.broadcasted_iota(jnp.int32, (sensors, sensors), 0) == lax.broadcasted_iota(
        jnp.int32, (sensors, sensors), 1
    )
    noise = jnp.sum(jnp.where(eye, noise_ref[...], 0.0), axis=1, keepdims=True)
    scale = 1.0 / jnp.sqrt(noise)
    for i in range(sensors // BLOCK):
        for j in range(width // BLOCK):
            part = map_ref[i * BLOCK : (i + 1) * BLOCK, j * BLOCK : (j + 1) * BLOCK]
            present = coupling_ref[i, j].astype(f32)
            hmat[i * BLOCK : (i + 1) * BLOCK, j * BLOCK : (j + 1) * BLOCK] = (
                part * present * scale[i * BLOCK : (i + 1) * BLOCK]
            )

    tick[0:8, :] = jnp.zeros((8, LANES), f32)
    diagonal = lax.broadcasted_iota(jnp.int32, (STAMP_DEV, LANES), 0) == lax.broadcasted_iota(
        jnp.int32, (STAMP_DEV, LANES), 1
    )
    for q in range(owners):
        picked = jnp.where(diagonal, rows_ref[q, 0:1, rows:], 0.0)
        tick[8 + q * STAMP_DEV : 8 + (q + 1) * STAMP_DEV, :] = jnp.broadcast_to(
            jnp.sum(picked, axis=1, keepdims=True), (STAMP_DEV, LANES)
        )

    def decays(q, carry):
        at = pl.multiple_of(q * STAMP_DEV, STAMP_DEV)
        here = tick[pl.ds(8 + at, STAMP_DEV), :]
        gap = here - pltpu.roll(tick[pl.ds(at, STAMP_DEV + 8), :], STAMP_DEV + 1, 0)[:STAMP_DEV]
        gap = jnp.concatenate([gap] * (width // LANES), axis=1)
        decay[pl.ds(at, STAMP_DEV), :] = jnp.exp(-rates_ref[...] * gap)
        return carry

    lax.fori_loop(0, owners, decays, 0)

    row_index = lax.broadcasted_iota(jnp.int32, (chunks * SENS_DEV, rows), 0)
    stamp_index = lax.broadcasted_iota(jnp.int32, (LANES, rows), 0)

    def collect(q, carry):
        cell = rows_ref[q, 0:1, :rows].astype(jnp.int32)
        value = rows_ref[q, 1:2, :rows]
        stamp_hot = jnp.where(stamp_index == (cell & (LANES - 1)), 1.0, 0.0).astype(bf16)
        mine = row_index == (cell >> 7)
        high = value.astype(bf16).astype(f32)
        features = jnp.concatenate(
            [
                jnp.where(mine, high, 0.0).astype(bf16),
                jnp.where(mine, value - high, 0.0).astype(bf16),
                jnp.where(mine, 1.0, 0.0).astype(bf16),
            ],
            axis=0,
        )
        got = lax.dot_general(
            features, stamp_hot, (((1,), (1,)), ((), ())), preferred_element_type=f32
        )
        count = chunks * SENS_DEV
        for c in range(chunks):
            at = pl.multiple_of(c * sensors + q * SENS_DEV, SENS_DEV)
            low = c * SENS_DEV
            sums[pl.ds(at, SENS_DEV), :] = (
                got[low : low + SENS_DEV] + got[count + low : count + low + SENS_DEV]
            )
            counts[pl.ds(at, SENS_DEV), :] = got[2 * count + low : 2 * count + low + SENS_DEV]
        return carry

    lax.fori_loop(0, owners, collect, 0)

    for c in range(chunks):
        number = counts[c * sensors : (c + 1) * sensors, :]
        observed = number > 0.0
        reading = sums[c * sensors : (c + 1) * sensors, :] / jnp.maximum(number, 1.0)
        reading = jnp.where(observed, reading, 0.0) * scale
        seen[c * sensors : (c + 1) * sensors, :] = jnp.where(observed, 1.0, 0.0).astype(bf16)
        pushed[c * LANES : (c + 1) * LANES, :] = prior_ref[...] * dot3(reading.T, hmat[...])

    below = lax.broadcasted_iota(jnp.int32, (sensors, sensors), 0) < lax.broadcasted_iota(
        jnp.int32, (sensors, sensors), 1
    )
    below = jnp.where(below, 1.0, 0.0).astype(bf16)
    table[...] = jnp.zeros(table.shape, jnp.int32)
    for c in range(chunks):
        observed = jnp.where(counts[c * sensors : (c + 1) * sensors, :] > 0.0, 1.0, 0.0)
        table[c : c + 1, :] = jnp.sum(observed, axis=0, keepdims=True).astype(jnp.int32)
        observed = observed.T
        place = dot(observed.astype(bf16), below)
        rank[c * LANES : (c + 1) * LANES, :] = jnp.where(observed > 0.0, place, 512.0)
    copy = pltpu.make_async_copy(table, scalars, arrived)
    copy.start()
    high, low = split(hmat[...])
    halves[:sensors, :] = high
    halves[sensors:, :] = low
    copy.wait()

    prior = jnp.broadcast_to(prior_ref[...], (8, width))
    sublane = lax.broadcasted_iota(jnp.int32, (LANES, LANES), 0)
    slot = lax.broadcasted_iota(jnp.int32, (KEPT, sensors), 0).astype(f32).astype(bf16)
    one, zero = jnp.ones((), bf16), jnp.zeros((), bf16)

    def fill(t, into):
        t = jnp.minimum(t, stamps - 1)
        at = pl.multiple_of((t // LANES) * sensors, sensors)
        pick = jnp.where(sublane == t % LANES, 1.0, 0.0).astype(bf16)
        into[...] = dot(seen[pl.ds(at, sensors), :], pick)

    def advance(t, moved, chosen, seen_now):
        base = moved + jnp.broadcast_to(pushed[pl.ds(t, 1), :], (8, width))
        after = jnp.broadcast_to(decay[pl.ds(jnp.minimum(t + 1, stamps - 1), 1), :], (8, width))
        base_after, prior_after = base * after, prior * after
        total = [jnp.zeros((8, width), f32) for _ in range(2)]
        matrix, start, rows_used = chosen
        for i in range(rows_used // 8):
            at = slice(start + 8 * i, start + 8 * i + 8)
            product = matrix[at, :] * moved
            product = (product[:, :128] + product[:, 128:256]) + (
                product[:, 256:384] + product[:, 384:]
            )
            weighted = jnp.broadcast_to(jnp.sum(product, axis=1, keepdims=True), (8, LANES))
            if seen_now is not None:
                weighted = weighted * seen_now[8 * i : 8 * i + 8, :]
            total[i % 2] = total[i % 2] + jnp.concatenate([weighted] * 4, axis=1) * matrix[at, :]
        change = total_over_sublanes(total[0] + total[1])
        states[pl.ds(t, 1), :] = (base - prior * change)[:1]
        return base_after - prior_after * change

    def prepare(group, into, steps=range(0, GROUP, BATCH)):
        first = pl.multiple_of(group * GROUP, GROUP)
        ranks = rank[pl.ds(first, GROUP), :]
        for j in steps:
            pick = jnp.concatenate(
                [
                    jnp.where(
                        slot == jnp.broadcast_to(ranks[j + k : j + k + 1], (KEPT, sensors)).astype(bf16),
                        one,
                        zero,
                    )
                    for k in range(BATCH)
                ],
                axis=0,
            )
            into[KEPT * j : KEPT * (j + BATCH), :] = dot(
                jnp.concatenate([pick, pick], axis=1), halves[...]
            )

    def on_all(group, moved, ahead):
        first = group * GROUP
        for j in range(GROUP):
            if ahead is not None and j % BATCH == 0:
                prepare(group + 1, ahead, (j,))
            if j + 1 < GROUP or ahead is None:
                fill(first + j + 1, seen_a if j % 2 else seen_b)
            moved = advance(
                first + j, moved, (hmat, 0, sensors), seen_b if j % 2 else seen_a
            )
        return moved

    def on_seen(group, moved, held, ahead):
        for j in range(GROUP):
            if ahead is not None and j % BATCH == 0:
                prepare(group + 1, ahead, (j,))
            moved = advance(group * GROUP + j, moved, (held, KEPT * j, KEPT), None)
        return moved

    def few_seen(group):
        most = jnp.int32(0)
        for j in range(GROUP):
            t = group * GROUP + j
            most = jnp.maximum(most, scalars[t // LANES, t % LANES])
        return most <= KEPT

    slab = slab_ref[0]
    last = (slab + 1) * (STAMP_DEV // GROUP)

    def step(group, moved, held, ahead):
        after = group + 1
        case = jnp.where(few_seen(group), 2, 0) + jnp.where(
            (after < last) & few_seen(jnp.minimum(after, stamps // GROUP - 1)), 1, 0
        )

        def branch(few, few_after):
            def run(moved):
                into = ahead if few_after else None
                if few:
                    if not few_after:
                        fill(after * GROUP, seen_a)
                    return on_seen(group, moved, held, into)
                return on_all(group, moved, into)

            return run

        return lax.switch(
            case, [branch(False, False), branch(False, True), branch(True, False), branch(True, True)], moved
        )

    def two_groups(k, moved):
        moved = step(2 * k, moved, held_a, held_b)
        return step(2 * k + 1, moved, held_b, held_a)

    prepare(jnp.int32(0), held_a)
    fill(jnp.int32(0), seen_a)
    moved = jnp.broadcast_to(x_ref[...] * decay[0:1, :], (8, width))
    lax.fori_loop(0, last // 2, two_groups, moved)
    out_ref[...] = states[pl.ds(pl.multiple_of(slab * STAMP_DEV, STAMP_DEV), STAMP_DEV), :]


def payload(slab_ref, offset_ref, sensor_ref, value_ref, ticks_ref, out_ref):
    copies, count = out_ref.shape[0], value_ref.shape[1]
    slab = slab_ref[...]
    per_chunk = LANES // STAMP_DEV
    chunk, within = slab // per_chunk, slab % per_chunk
    cell = (chunk * SENS_DEV + sensor_ref[...]) * LANES + within * STAMP_DEV + offset_ref[...]
    cell, value = cell.astype(f32), value_ref[...]
    tick = jnp.concatenate(
        [ticks_ref[...].astype(f32), jnp.zeros((1, LANES - STAMP_DEV), f32)], axis=1
    )
    for d in range(copies):
        out_ref[d, 0:1, :count] = cell
        out_ref[d, 1:2, :count] = value
        out_ref[d, 0:1, count:] = tick
        out_ref[d, 1:2, count:] = jnp.zeros((1, LANES), f32)


def shards(
    x_start,
    ticks,
    rates,
    sensor_map,
    coupling,
    prior_var,
    noise_var,
    read_slab,
    read_offset,
    read_sensor,
    read_value,
):
    slab = lax.axis_index("tm").astype(jnp.int32)
    owners = lax.axis_size("tm")
    sensors, width = sensor_map.shape
    count = read_value.shape[0]
    copies = pl.pallas_call(
        payload,
        out_shape=jax.ShapeDtypeStruct((owners, 2, count + LANES), f32),
    )(
        read_slab.reshape(1, count),
        read_offset[None],
        read_sensor[None],
        read_value[None],
        ticks[None],
    )
    rows = lax.all_to_all(copies, "tm", split_axis=0, concat_axis=0, tiled=True)
    stamps = owners * STAMP_DEV
    chunks = stamps // LANES
    vmem, smem = pl.BlockSpec(memory_space=pltpu.VMEM), pl.BlockSpec(memory_space=pltpu.SMEM)
    return pl.pallas_call(
        kernel,
        out_shape=jax.ShapeDtypeStruct((STAMP_DEV, width), f32),
        in_specs=[smem, smem] + [vmem] * 6,
        out_specs=vmem,
        scratch_shapes=[
            pltpu.VMEM((sensors, width), f32),
            pltpu.VMEM((chunks * sensors, LANES), f32),
            pltpu.VMEM((chunks * sensors, LANES), f32),
            pltpu.VMEM((chunks * sensors, LANES), bf16),
            pltpu.VMEM((stamps, width), f32),
            pltpu.VMEM((stamps, width), f32),
            pltpu.VMEM((stamps + 8, LANES), f32),
            pltpu.VMEM((stamps, width), f32),
            pltpu.VMEM((sensors, LANES), f32),
            pltpu.VMEM((sensors, LANES), f32),
            pltpu.VMEM((stamps, sensors), f32),
            pltpu.VMEM((8, LANES), jnp.int32),
            pltpu.SMEM((8, LANES), jnp.int32),
            pltpu.SemaphoreType.DMA,
            pltpu.VMEM((2 * sensors, width), bf16),
            pltpu.VMEM((GROUP * KEPT, width), f32),
            pltpu.VMEM((GROUP * KEPT, width), f32),
        ],
        compiler_params=pltpu.CompilerParams(vmem_limit_bytes=40 * 2**20),
    )(
        slab[None],
        coupling,
        rows,
        x_start[None],
        rates[None],
        sensor_map,
        prior_var[None],
        noise_var[None],
    )


def solution(mesh):
    return jax.shard_map(
        shards,
        mesh=mesh,
        in_specs=(
            P("region"),
            P(("region", "tm")),
            P("region"),
            P("region", None),
            P("region", None),
            P("region"),
            P("region"),
            P(("region", "tm"), None),
            P(("region", "tm")),
            P(("region", "tm")),
            P(("region", "tm")),
        ),
        out_specs=P(("region", "tm"), None),
        check_vma=False,
    )
```
